32 devices in a mesh: groups: 2 (over y), rows: 4 (over z), cols: 2 (over x), sub: 2 (over core).
Axes of the slice: x: 2, y: 2, z: 4, core: 2. Of those that a mesh axis runs over, the one named last changes fastest.
Arguments:
- features: float32 [2048, 8192], P(('groups', 'rows'), ('cols', 'sub')), parts along dimension 0, may hold values from -6 to 6
Outputs:
- reduced: float32 [2048, 8192], P(('groups', 'rows'), ('cols', 'sub')), parts along dimension 0
The draws below stay inside these ranges and needn't reach their ends.
There are 2 independent parts, one for each index of `groups`. The reference program is written for one: setup_inputs(seed, part) draws one part's arguments, and reference() takes and returns one part's arrays. A program takes and returns all parts, laid end to end along the dimension named above; each array names one. Nothing has to cross between parts.
All inputs are finite; a program needn't handle non-finite values.
Results may differ from the reference program's by a relative error of at most 0.0003.
Values sent between devices are 32-bit elements; how exact they have to be, the bound alone decides.
A program may use at most 64 MiB of HBM per device.

```python
import math
import jax
import jax.numpy as jnp
from jax import lax

WIDTH = 8192
BLOCK = 256
PIVOTS = 3
TOKENS = 1024


def block_levels(rng, dims, cuts, least, largest):
    def one(dim, blocks):
        draws = jax.random.uniform(jax.random.fold_in(jax.random.fold_in(rng, 6), dim), (blocks,), jnp.float32, least / len(cuts), largest / len(cuts))
        return jnp.repeat(jnp.exp(draws), dims[dim] // blocks).reshape((-1,) + (1,) * (len(dims) - dim - 1))

    gain = one(*cuts[0])
    for cut in cuts[1:]:
        gain = gain * one(*cut)
    return gain


def noise(stream_key, extent, deviation, reach, pieces=(), kind=jnp.bfloat16):
    array = jax.random.normal(stream_key, extent, jnp.float32) * deviation
    if len(pieces) > 0:
        array = block_levels(stream_key, extent, pieces, -0.22, 0.18) * array
    return jnp.clip(array, min=-reach, max=reach).astype(kind)


def setup_inputs(seed: int = 0, part: int = 0) -> dict:
    keys = jax.random.split(jax.random.key(seed), 2)
    part_keys = jax.random.split(jax.random.fold_in(keys[1], part), 2)
    features = noise(part_keys[0], (TOKENS, WIDTH), 1.0, 6.0, ((0, 4), (1, 4)), jnp.float32)
    return dict(features=features)


def reference(features):
    scale = math.sqrt(TOKENS)
    current = features
    for pivot_index in range(PIVOTS):
        start_col = pivot_index * BLOCK
        end_col = start_col + BLOCK
        raw_block = current[:, start_col:end_col]
        target = current[:, start_col:]
        raw_sums = jnp.dot(raw_block.T.astype(jnp.float32), target.astype(jnp.float32), precision=lax.Precision.HIGHEST, preferred_element_type=jnp.float32)
        gram_sum = raw_sums[:, :BLOCK]
        lower_factor = jnp.linalg.cholesky(gram_sum)
        ortho = scale * lax.linalg.triangular_solve(lower_factor, raw_block, left_side=False, lower=True, transpose_a=True)
        coeffs = scale * lax.linalg.triangular_solve(lower_factor, raw_sums[:, BLOCK:], left_side=True, lower=True)
        later = current[:, end_col:] - jnp.dot(ortho.astype(jnp.float32), coeffs.astype(jnp.float32), precision=lax.Precision.HIGHEST, preferred_element_type=jnp.float32) / TOKENS
        current = jnp.concatenate([current[:, :start_col], ortho, later], axis=1)
    return current
```

```python
import functools
import math

import jax
import jax.numpy as jnp
from jax import lax
from jax.experimental import pallas as pl
from jax.experimental.pallas import tpu as pltpu
from jax.sharding import PartitionSpec as P

BLOCK = 256
PIVOTS = 3
LEAF = 128
GROUP = 8
HIGHEST = lax.Precision.HIGHEST


def dot(a, b, contract, precision=HIGHEST):
    return lax.dot_general(
        a, b, (contract, ((), ())), precision=precision, preferred_element_type=jnp.float32
    )


def leaf_inverse(block):
    size = block.shape[0]
    done = []
    rest = block
    for first in range(0, size, GROUP):
        rows = size - first
        row = lax.broadcasted_iota(jnp.int32, (rows, size), 0)
        lane = lax.broadcasted_iota(jnp.int32, (rows, size), 1)
        cols = [
            jnp.broadcast_to(rest[:, first + p : first + p + 1], (rows, size))
            for p in range(GROUP)
        ]
        inside = (lane >= first) & (lane < first + GROUP)
        rest = jnp.where(inside, (lane == row + first).astype(jnp.float32), rest)
        top_row = lax.broadcasted_iota(jnp.int32, (GROUP, size), 0)
        gain = jnp.zeros((GROUP, size), jnp.float32)
        for p in range(GROUP):
            pivot = cols[p][p : p + 1, :]
            factor = jnp.where(row > p, cols[p] * (1.0 / pivot), 0.0)
            gain = jnp.where(top_row == p, lax.rsqrt(pivot), gain)
            for q in range(p + 1, GROUP):
                cols[q] = cols[q] - factor * cols[q][p : p + 1, :]
            rest = rest - factor * rest[p : p + 1, :]
        done.append(rest[:GROUP] * gain)
        rest = rest[GROUP:]
    full = jnp.concatenate(done, axis=0)
    row = lax.broadcasted_iota(jnp.int32, (size, size), 0)
    lane = lax.broadcasted_iota(jnp.int32, (size, size), 1)
    return jnp.where(row >= lane, full, 0.0)


def factor_kernel(gram_ref, inv_ref, work, low):
    total = gram_ref.shape[0]
    count = total // LEAF
    work[...] = gram_ref[...]
    inv_ref[...] = jnp.zeros_like(inv_ref)

    for j in range(count):
        a, b = j * LEAF, (j + 1) * LEAF
        leaf = leaf_inverse(work[a:b, a:b])
        if j > 0:
            mixed = dot(low[a:b, :a], inv_ref[:a, :a], ((1,), (0,)))
            inv_ref[a:b, :a] = -dot(leaf, mixed, ((1,), (0,)))
        inv_ref[a:b, a:b] = leaf
        if b < total:
            panel = dot(work[b:, a:b], leaf, ((1,), (1,)))
            low[b:, a:b] = panel
            work[b:, b:] = work[b:, b:] - dot(panel, panel, ((1,), (1,)))


def inverse_factor(gram):
    size = gram.shape[0]
    return pl.pallas_call(
        factor_kernel,
        out_shape=jax.ShapeDtypeStruct((size, size), jnp.float32),
        in_specs=[pl.BlockSpec(memory_space=pltpu.VMEM)],
        out_specs=pl.BlockSpec(memory_space=pltpu.VMEM),
        scratch_shapes=[pltpu.VMEM((size, size), jnp.float32)] * 2,
        compiler_params=pltpu.CompilerParams(vmem_limit_bytes=32 * 1024 * 1024),
        cost_estimate=pl.CostEstimate(
            flops=60 * 10**9, bytes_accessed=8 * size * size, transcendentals=0
        ),
    )(gram)


def local(features):
    rows_here, cols_here = features.shape
    span = PIVOTS * BLOCK
    col_index = lax.axis_index(("cols", "sub"))
    row_index = lax.axis_index("rows")
    tokens = rows_here * lax.axis_size("rows")
    scale = math.sqrt(tokens)
    own = features[:, :span]
    kept = jnp.where(col_index == 0, own, 0.0)
    mine = lax.psum(kept, ("cols", "sub"))
    pivots = lax.all_gather(mine, "rows", axis=0, tiled=True)
    moved = lax.all_to_all(features, "rows", split_axis=1, concat_axis=0, tiled=True)
    gram = dot(pivots, pivots, ((0,), (0,)))
    inverse = inverse_factor(gram)
    ortho = scale * dot(mine, inverse, ((1,), (1,)))
    raw = dot(pivots, moved, ((0,), (0,)))
    mixing = dot(inverse, dot(inverse, raw, ((1,), (0,))), ((0,), (0,)))
    later = moved - dot(pivots, mixing, ((1,), (0,)))
    back = lax.all_to_all(later, "rows", split_axis=0, concat_axis=1, tiled=True)
    head = jnp.where(col_index == 0, ortho, back[:, :span])
    return jnp.concatenate([head, back[:, span:]], axis=1)


def solution(mesh):
    spec = P(("groups", "rows"), ("cols", "sub"))
    return jax.shard_map(local, mesh=mesh, in_specs=(spec,), out_specs=spec, check_vma=False)
```

```python
import functools
import math

import jax
import jax.numpy as jnp
from jax import lax
from jax.experimental import pallas as pl
from jax.experimental.pallas import tpu as pltpu
from jax.sharding import PartitionSpec as P

BLOCK = 256
PIVOTS = 3
LEAF = 128
GROUP = 8
HIGHEST = lax.Precision.HIGHEST


def dot(a, b, contract, precision=HIGHEST):
    return lax.dot_general(
        a, b, (contract, ((), ())), precision=precision, preferred_element_type=jnp.float32
    )


def leaf_inverse(block):
    size = block.shape[0]
    done = []
    rest = block
    for first in range(0, size, GROUP):
        rows = size - first
        row = lax.broadcasted_iota(jnp.int32, (rows, size), 0)
        lane = lax.broadcasted_iota(jnp.int32, (rows, size), 1)
        cols = [
            jnp.broadcast_to(rest[:, first + p : first + p + 1], (rows, size))
            for p in range(GROUP)
        ]
        inside = (lane >= first) & (lane < first + GROUP)
        rest = jnp.where(inside, (lane == row + first).astype(jnp.float32), rest)
        top_row = lax.broadcasted_iota(jnp.int32, (GROUP, size), 0)
        gain = jnp.zeros((GROUP, size), jnp.float32)
        for p in range(GROUP):
            pivot = cols[p][p : p + 1, :]
            factor = jnp.where(row > p, cols[p] * (1.0 / pivot), 0.0)
            gain = jnp.where(top_row == p, lax.rsqrt(pivot), gain)
            for q in range(p + 1, GROUP):
                cols[q] = cols[q] - factor * cols[q][p : p + 1, :]
            rest = rest - factor * rest[p : p + 1, :]
        done.append(rest[:GROUP] * gain)
        rest = rest[GROUP:]
    full = jnp.concatenate(done, axis=0)
    row = lax.broadcasted_iota(jnp.int32, (size, size), 0)
    lane = lax.broadcasted_iota(jnp.int32, (size, size), 1)
    return jnp.where(row >= lane, full, 0.0)


def factor_kernel(gram_ref, inv_ref, work, low):
    total = gram_ref.shape[0]
    count = total // LEAF
    work[...] = gram_ref[...]
    inv_ref[...] = jnp.zeros_like(inv_ref)

    for j in range(count):
        a, b = j * LEAF, (j + 1) * LEAF
        leaf = leaf_inverse(work[a:b, a:b])
        if j > 0:
            mixed = dot(low[a:b, :a], inv_ref[:a, :a], ((1,), (0,)))
            inv_ref[a:b, :a] = -dot(leaf, mixed, ((1,), (0,)))
        inv_ref[a:b, a:b] = leaf
        if b < total:
            panel = dot(work[b:, a:b], leaf, ((1,), (1,)))
            low[b:, a:b] = panel
            work[b:, b:] = work[b:, b:] - dot(panel, panel, ((1,), (1,)))


def inverse_factor(gram):
    size = gram.shape[0]
    return pl.pallas_call(
        factor_kernel,
        out_shape=jax.ShapeDtypeStruct((size, size), jnp.float32),
        in_specs=[pl.BlockSpec(memory_space=pltpu.VMEM)],
        out_specs=pl.BlockSpec(memory_space=pltpu.VMEM),
        scratch_shapes=[pltpu.VMEM((size, size), jnp.float32)] * 2,
        compiler_params=pltpu.CompilerParams(vmem_limit_bytes=32 * 1024 * 1024),
        cost_estimate=pl.CostEstimate(
            flops=60 * 10**9, bytes_accessed=8 * size * size, transcendentals=0
        ),
    )(gram)


def device(rows, cols, sub):
    return (lax.axis_index("groups"), rows, cols, sub)


def remote(src, dst, send, recv, target):
    return pltpu.make_async_remote_copy(
        src_ref=src,
        dst_ref=dst,
        send_sem=send,
        recv_sem=recv,
        device_id=target,
        device_id_type=pl.DeviceIdType.MESH,
    )


def greet(targets):
    barrier = pltpu.get_barrier_semaphore()
    for target in targets:
        pl.semaphore_signal(
            barrier, inc=1, device_id=target, device_id_type=pl.DeviceIdType.MESH
        )
    pl.semaphore_wait(barrier, len(targets))


def gather_kernel(
    ring, feat_ref, full_ref, own_sem, s0, r0, sz, rz, sx, rx, sc, rc
):
    z, x, c = (lax.axis_index(name) for name in ("rows", "cols", "sub"))
    rows_here = feat_ref.shape[0]
    span = full_ref.shape[1]
    part = rows_here // 4
    q = 2 * x + c
    peers = [device(lax.rem(z + d, ring), x, c) for d in range(1, ring)]
    x_peer, c_peer, xc_peer = device(z, 1 - x, c), device(z, x, 1 - c), device(z, 1 - x, 1 - c)
    greet(peers + [x_peer, c_peer, xc_peer])

    def piece(zz, quarter):
        return full_ref.at[pl.ds(pl.multiple_of(zz * rows_here + quarter * part, 8), part), :]

    def seed(n, xx, cc):
        quarter = 2 * xx + cc
        src = feat_ref.at[quarter * part : (quarter + 1) * part, :span]
        return remote(src, piece(z, quarter), s0.at[n], r0, device(z, xx, cc))

    seeds = [seed(0, 1, 0), seed(1, 1, 1), seed(2, 0, 1)]
    local_copy = pltpu.make_async_copy(feat_ref.at[:part, :span], piece(z, 0), own_sem)

    @pl.when(q == 0)
    def _():
        for copy in seeds:
            copy.start()
        local_copy.start()
        local_copy.wait()

    @pl.when(q != 0)
    def _():
        remote(piece(z, q), piece(z, q), s0.at[0], r0, c_peer).wait_recv()

    other = 2 * (1 - x) + c
    order = [1, ring - 1] + list(range(2, ring - 1))
    sends = []
    for d in order:
        sends.append(
            remote(piece(z, q), piece(z, q), sz.at[d], rz.at[d], peers[d - 1])
        )
        sends[-1].start()

    def spread(d, zz):
        for copy in (
            remote(piece(zz, q), piece(zz, q), sx.at[d], rx.at[d], x_peer),
            remote(piece(zz, q), piece(zz, q), sc.at[d], rc.at[d], c_peer),
        ):
            copy.start()
            sends.append(copy)

    def hand_on(d, zz):
        remote(piece(zz, other), piece(zz, other), sx.at[d], rx.at[d], x_peer).wait_recv()
        copy = remote(
            piece(zz, other), piece(zz, other), sc.at[ring + d], rc.at[ring + d], c_peer
        )
        copy.start()
        sends.append(copy)

    spread(0, z)
    for d in order:
        zz = lax.rem(z - d + ring, ring)
        remote(piece(zz, q), piece(zz, q), sz.at[d], rz.at[d], c_peer).wait_recv()
        spread(d, zz)
    for d in [0] + order:
        hand_on(d, lax.rem(z - d + ring, ring))
    mate, far = 2 * x + (1 - c), 2 * (1 - x) + (1 - c)
    for d in [0] + order:
        zz = lax.rem(z - d + ring, ring)
        remote(piece(zz, mate), piece(zz, mate), sc.at[d], rc.at[d], c_peer).wait_recv()
        remote(
            piece(zz, far), piece(zz, far), sc.at[ring + d], rc.at[ring + d], c_peer
        ).wait_recv()
    for copy in sends:
        copy.wait_send()

    @pl.when(q == 0)
    def _():
        for copy in seeds:
            copy.wait_send()


def gather_pivots(features, span, ring):
    rows_here = features.shape[0]
    dma = pltpu.SemaphoreType.DMA
    return pl.pallas_call(
        functools.partial(gather_kernel, ring),
        out_shape=jax.ShapeDtypeStruct((rows_here * ring, span), jnp.float32),
        in_specs=[pl.BlockSpec(memory_space=pl.ANY)],
        out_specs=pl.BlockSpec(memory_space=pl.ANY),
        scratch_shapes=[
            dma(()), dma((3,)), dma(()),
            dma((ring,)), dma((ring,)),
            dma((ring,)), dma((ring,)),
            dma((2 * ring,)), dma((2 * ring,)),
        ],
        compiler_params=pltpu.CompilerParams(collective_id=0, has_side_effects=True),
    )(features)


def return_kernel(ring, later_ref, out_ref, own_sem, send, recv):
    z, x, c = (lax.axis_index(name) for name in ("rows", "cols", "sub"))
    rows_here = out_ref.shape[0]
    width = later_ref.shape[1]
    peers = [device(lax.rem(z + d, ring), x, c) for d in range(1, ring)]
    greet(peers)

    def rows_of(zz):
        return later_ref.at[pl.ds(pl.multiple_of(zz * rows_here, 8), rows_here), :]

    def cols_of(zz):
        return out_ref.at[:, pl.ds(pl.multiple_of(zz * width, 128), width)]

    sends = []
    for d in [2, 1, 3] if ring == 4 else range(1, ring):
        to = lax.rem(z + d, ring)
        copy = remote(rows_of(to), cols_of(z), send.at[d], recv.at[d], peers[d - 1])
        copy.start()
        sends.append(copy)
    own = pltpu.make_async_copy(rows_of(z), cols_of(z), own_sem)
    own.start()
    own.wait()
    for d in range(1, ring):
        zz = lax.rem(z - d + ring, ring)
        remote(rows_of(zz), cols_of(zz), send.at[d], recv.at[d], peers[d - 1]).wait_recv()
    for copy in sends:
        copy.wait_send()


def send_back(later, rows_here, ring):
    width = later.shape[1]
    dma = pltpu.SemaphoreType.DMA
    return pl.pallas_call(
        functools.partial(return_kernel, ring),
        out_shape=jax.ShapeDtypeStruct((rows_here, width * ring), jnp.float32),
        in_specs=[pl.BlockSpec(memory_space=pl.ANY)],
        out_specs=pl.BlockSpec(memory_space=pl.ANY),
        scratch_shapes=[dma(()), dma((ring,)), dma((ring,))],
        compiler_params=pltpu.CompilerParams(collective_id=1, has_side_effects=True),
    )(later)


def local_near(features):
    rows_here, cols_here = features.shape
    span = PIVOTS * BLOCK
    ring = lax.axis_size("rows")
    col_index = lax.axis_index(("cols", "sub"))
    row_index = lax.axis_index("rows")
    tokens = rows_here * ring
    width = cols_here // ring
    pivots = gather_pivots(features, span, ring)
    features, pivots = lax.optimization_barrier((features, pivots))
    moved = lax.all_to_all(features, "rows", split_axis=1, concat_axis=0, tiled=True)
    gram = dot(pivots, pivots, ((0,), (0,)))
    inverse = inverse_factor(gram)
    high = lax.Precision.HIGH
    basis = dot(pivots, inverse, ((1,), (1,)))
    project = jnp.eye(tokens, dtype=jnp.float32) - dot(basis, basis, ((1,), (1,)), high)
    padded = jnp.pad(inverse, ((0, cols_here - span), (0, 0)))
    chosen = lax.dynamic_slice(padded, (row_index * width, 0), (width, span))
    ortho = math.sqrt(tokens) * dot(pivots, chosen, ((1,), (1,)))
    column = row_index * width + jnp.arange(width, dtype=jnp.int32)
    pivot_here = (column < span) & (col_index == 0)
    later = dot(project, moved, ((1,), (0,)), high)
    later = jnp.where(pivot_here[None, :], ortho, later)
    return send_back(later, rows_here, ring)


def local(features):
    rows_here, cols_here = features.shape
    span = PIVOTS * BLOCK
    col_index = lax.axis_index(("cols", "sub"))
    tokens = rows_here * lax.axis_size("rows")
    scale = math.sqrt(tokens)
    own = features[:, :span]
    kept = jnp.where(col_index == 0, own, 0.0)
    mine = lax.psum(kept, ("cols", "sub"))
    pivots = lax.all_gather(mine, "rows", axis=0, tiled=True)
    moved = lax.all_to_all(features, "rows", split_axis=1, concat_axis=0, tiled=True)
    gram = dot(pivots, pivots, ((0,), (0,)))
    inverse = inverse_factor(gram)
    ortho = scale * dot(mine, inverse, ((1,), (1,)))
    raw = dot(pivots, moved, ((0,), (0,)))
    mixing = dot(inverse, dot(inverse, raw, ((1,), (0,))), ((0,), (0,)))
    later = moved - dot(pivots, mixing, ((1,), (0,)))
    back = lax.all_to_all(later, "rows", split_axis=0, concat_axis=1, tiled=True)
    head = jnp.where(col_index == 0, ortho, back[:, :span])
    return jnp.concatenate([head, back[:, span:]], axis=1)


def solution(mesh):
    spec = P(("groups", "rows"), ("cols", "sub"))
    near = mesh.shape["cols"] == 2 and mesh.shape["sub"] == 2 and mesh.shape["rows"] == 4

    def body(features):
        rows_here, cols_here = features.shape
        fits = rows_here % 32 == 0 and cols_here % (128 * mesh.shape["rows"]) == 0
        if near and fits and cols_here >= PIVOTS * BLOCK:
            return local_near(features)
        return local(features)

    return jax.shard_map(body, mesh=mesh, in_specs=(spec,), out_specs=spec, check_vma=False)
```
